32 devices in a mesh: space: 8 (over y, x, core), chan: 4 (over z).
Axes of the slice: x: 2, y: 2, z: 4, core: 2. Of those that a mesh axis runs over, the one named last changes fastest.
Arguments:
- field: bfloat16 [96, 768, 32], P('chan', 'space'), may hold values from -6 to 6
- grad_out: bfloat16 [96, 768, 32], P('chan', 'space'), may hold values from -6 to 6
- filters: bfloat16 [9, 96, 96], replicated, may hold values from -0.21875 to 0.21875
Outputs:
- grad_field: float32 [96, 768, 32], P('chan', 'space')
- grad_filters: float32 [9, 96, 96], P(None, 'chan')
The draws below stay inside these ranges and needn't reach their ends.
All inputs are finite; a program needn't handle non-finite values.
Results may differ from the reference program's by a relative error of at most 0.0003.
Values may be sent and summed in bfloat16 or wider, within the bound.
A program may use at most 64 MiB of HBM per device.

```python
import math
import jax
import jax.numpy as jnp
from jax import lax

CH = 96
COL_DEV = 96
COLS = 768
ROWS = 32


def block_scale(key, dims, cuts, smallest, largest):
    def one(axis_at, blocks):
        draws = jax.random.uniform(jax.random.fold_in(jax.random.fold_in(key, 6), axis_at), (blocks,), jnp.float32, smallest / len(cuts), largest / len(cuts))
        return jnp.repeat(jnp.exp(draws), dims[axis_at] // blocks).reshape((-1,) + (1,) * (len(dims) - axis_at - 1))

    level = one(*cuts[0])
    for cut in cuts[1:]:
        level = level * one(*cut)
    return level


def centred(stream_key, shape, spread, bound, shards=(), kind=jnp.bfloat16):
    values = spread * jax.random.normal(stream_key, shape, jnp.float32)
    if shards:
        values = values * block_scale(stream_key, shape, shards, -0.22, 0.18)
    return jnp.clip(values, -bound, bound).astype(kind)


def setup_inputs(seed: int = 0) -> dict:
    arg_keys = jax.random.split(jax.random.key(seed), 4)
    field = centred(arg_keys[0], (CH, COLS, ROWS), 1.0, 6.0, ((0, 4), (1, 8)))
    grad_out = centred(arg_keys[1], (CH, COLS, ROWS), 1.0, 6.0, ((0, 4), (1, 8)))
    filters = centred(arg_keys[2], (9, CH, CH), (9 * CH) ** -0.5, 0.21875)
    return {"field": field, "grad_out": grad_out, "filters": filters}


def reference(field, grad_out, filters):
    chans, cols_all, rows = field.shape
    padded = jnp.pad(grad_out, ((0, 0), (2, 2), (2, 2)))
    weights = filters.astype(jnp.float32)
    blocks = cols_all // COL_DEV

    def step(acc, index):
        begin = (index * COL_DEV).astype(jnp.int32)
        x_blk = lax.dynamic_slice_in_dim(field, begin, COL_DEV, 1).astype(jnp.float32)
        g_blk = lax.dynamic_slice_in_dim(padded, begin, COL_DEV + 4, 1).astype(jnp.float32)
        result = jnp.zeros((chans, COL_DEV, rows), jnp.float32)
        parts = []
        for a in range(3):
            for b in range(3):
                k = a * 3 + b
                shifted = g_blk[:, 4 - 2 * a:4 - 2 * a + COL_DEV, 4 - 2 * b:4 - 2 * b + rows]
                result = result + jnp.einsum('io,owr->iwr', weights[k], shifted, precision=lax.Precision.HIGHEST)
                parts.append(jnp.einsum('iwr,owr->io', x_blk, shifted, precision=lax.Precision.HIGHEST))
        return (acc + jnp.stack(parts), result)
    total, pieces = lax.scan(step, jnp.zeros((9, chans, chans), jnp.float32), jnp.arange(blocks, dtype=jnp.int32))
    grad_field = jnp.transpose(pieces, (1, 0, 2, 3)).reshape(chans, cols_all, rows)
    return (grad_field, total * (1.0 / math.sqrt(rows * cols_all)))
```

```python
import functools
import math

import jax
import jax.numpy as jnp
from jax import lax
from jax.experimental import pallas as pl
from jax.experimental.pallas import tpu as pltpu
from jax.sharding import PartitionSpec as P

MESH = pl.DeviceIdType.MESH
F32 = jnp.float32
BF16 = jnp.bfloat16
LANES = 128
PAD = 32


def lane_index(shape):
    return lax.broadcasted_iota(jnp.int32, shape, len(shape) - 1)


def roll(x, shift):
    return pltpu.roll(x, shift % LANES, x.ndim - 1)


def row_pad(x):
    rows, chans, lanes = x.shape
    return jnp.concatenate([x, jnp.zeros((rows, PAD - chans, lanes), x.dtype)], axis=1)


def kernel(
    ns, nc, scale,
    field_ref, grad_ref, filt_ref, gf_ref, gw_ref,
    wide, wire, halo_own, halo_in, g, fa, wm, parts, rs, total,
    z_send, z_recv, h_send, h_recv, rs_send, rs_recv, ag_send, ag_recv,
):
    s = lax.axis_index("space")
    c = lax.axis_index("chan")
    chans, rows, cols = field_ref.shape
    wire_rows = rows * cols // LANES
    half = wire_rows // 2
    nq = nc * PAD
    has_left, has_right = s > 0, s < ns - 1
    has_below, has_above = c > 0, c < nc - 1

    barrier = pltpu.get_barrier_semaphore()

    def greet(space, chan):
        pl.semaphore_signal(
            barrier, inc=1, device_id={"space": space, "chan": chan}, device_id_type=MESH
        )

    for d in range(1, ns):
        greet(lax.rem(s + d, ns), c)
    for d in range(1, nc):
        other = lax.rem(c + d, nc)

        @pl.when(has_left)
        def _():
            greet(s - 1, other)

        @pl.when(has_right)
        def _():
            greet(s + 1, other)

    @pl.when(has_below)
    def _():
        greet(s, c - 1)

    @pl.when(has_above)
    def _():
        greet(s, c + 1)

    wide[...] = jnp.zeros_like(wide)
    wide[:, :, :cols] = grad_ref[...].astype(F32)
    x = wide[...]
    lane = lane_index((chans, 8, LANES))
    tail = x[:, wire_rows:, :]
    packed = jnp.concatenate(
        [
            jnp.where(lane < cols, x[:, 8 * t : 8 * t + 8, :], roll(tail, cols - 32 * t))
            for t in range(wire_rows // 8)
        ],
        axis=1,
    )
    packed = jnp.swapaxes(packed, 0, 1)
    for h in range(2):
        wire[c, h] = packed[h * half : (h + 1) * half].reshape(half * chans, LANES).astype(BF16)

    lane = lane_index(x.shape)
    y = jnp.where(lane < 2, x, 0.0) + roll(
        jnp.where((lane >= cols - 2) & (lane < cols), x, 0.0), 30 - (cols - 2)
    )
    y = jnp.swapaxes(y, 0, 1)
    count = rows
    while count > 1:
        count //= 2
        y = y[:count] + roll(y[count:], 4 * count)
    halo_own[...] = row_pad(y)[0].astype(BF16)

    greeted = (ns - 1) + (nc - 1) * (
        has_left.astype(jnp.int32) + has_right.astype(jnp.int32)
    ) + has_below.astype(jnp.int32) + has_above.astype(jnp.int32)
    pl.semaphore_wait(barrier, greeted)

    def z_copy(up, t, h):
        block = c - t if up else c + t
        way = 0 if up else 1
        return pltpu.make_async_remote_copy(
            src_ref=wire.at[block, h],
            dst_ref=wire.at[block, h],
            send_sem=z_send.at[way, t, h],
            recv_sem=z_recv.at[way, t, h],
            device_id={"space": s, "chan": c + 1 if up else c - 1},
            device_id_type=MESH,
        )

    def z_arrival(up, t, h):
        block = c - 1 - t if up else c + 1 + t
        way = 0 if up else 1
        return pltpu.make_async_remote_copy(
            src_ref=wire.at[block, h],
            dst_ref=wire.at[block, h],
            send_sem=z_send.at[way, t, h],
            recv_sem=z_recv.at[way, t, h],
            device_id={"space": s, "chan": c - 1 if up else c + 1},
            device_id_type=MESH,
        )

    def sends(up, t):
        if up:
            return has_above & (c - t >= 0)
        return has_below & (c + t < nc)

    def arrives(up, t):
        if up:
            return c - 1 - t >= 0
        return c + 1 + t < nc

    def halo_copy(right, chan):
        side = 0 if right else 1
        return pltpu.make_async_remote_copy(
            src_ref=halo_own,
            dst_ref=halo_in.at[side, c],
            send_sem=h_send.at[side, chan],
            recv_sem=h_recv.at[side, c],
            device_id={"space": s + 1 if right else s - 1, "chan": chan},
            device_id_type=MESH,
        )

    def halo_arrival(side, block):
        return pltpu.make_async_remote_copy(
            src_ref=halo_own,
            dst_ref=halo_in.at[side, block],
            send_sem=h_send.at[side, block],
            recv_sem=h_recv.at[side, block],
            device_id={"space": s - 1 if side == 0 else s + 1, "chan": block},
            device_id_type=MESH,
        )

    for h in range(2):
        for up in (True, False):

            @pl.when(sends(up, 0))
            def _():
                z_copy(up, 0, h).start()

    for right, there in ((True, has_right), (False, has_left)):

        @pl.when(there)
        def _():
            for chan in range(nc):
                halo_copy(right, chan).start()

    for side, there in ((0, has_left), (1, has_right)):

        @pl.when(jnp.logical_not(there))
        def _():
            halo_in[side] = jnp.zeros_like(halo_in[side])

    wide[:, :, :cols] = field_ref[...].astype(F32)
    f = jnp.swapaxes(wide[...], 0, 1)
    fa[...] = jnp.zeros_like(fa)
    for a in range(3):
        fa[a, 2 : 2 + rows] = row_pad(roll(f, -2 * (a - 1))).astype(BF16)

    ch = filt_ref.shape[1]
    mine = lax.broadcasted_iota(jnp.int32, (chans, ch), 0) + c * chans
    pick = (mine == lane_index((chans, ch))).astype(F32).astype(BF16)
    q = lane_index((ch, nq))
    from_q = (q // PAD) * chans + lax.rem(q, PAD)
    spread = (
        (from_q == lax.broadcasted_iota(jnp.int32, (ch, nq), 0)) & (lax.rem(q, PAD) < chans)
    ).astype(F32).astype(BF16)
    taps = [
        jnp.dot(pick, filt_ref[k], preferred_element_type=F32) for k in range(9)
    ]
    taps = jnp.concatenate(taps, axis=0).astype(BF16)
    taps = jnp.dot(taps, spread, preferred_element_type=F32)
    wm[...] = jnp.concatenate(
        [
            jnp.concatenate(
                [taps[(3 * a + b) * chans : (3 * a + b + 1) * chans] for a in range(3)], axis=0
            )
            for b in range(3)
        ],
        axis=1,
    ).astype(BF16)

    for block in range(nc):
        g[block, 0:2] = jnp.zeros((2, PAD, LANES), BF16)
        g[block, rows + 2 :] = jnp.zeros((2, PAD, LANES), BF16)

    def unpack(block):
        for side, there in ((0, has_left), (1, has_right)):

            @pl.when(there)
            def _():
                halo_arrival(side, block).wait_recv()

        w = jnp.concatenate(
            [wire[block, h].astype(F32).reshape(half, chans, LANES) for h in range(2)], axis=0
        )
        lane = lane_index((chans, LANES))
        left = halo_in[0, block].astype(F32)[:chans]
        right = halo_in[1, block].astype(F32)[:chans]
        border = jnp.where(lane % 4 < 2, right, left)
        edge = ((lane >= cols) & (lane < cols + 2)) | (lane >= LANES - 2)
        out = []
        for r in range(rows):
            if r < wire_rows:
                main = w[r]
            else:
                j = r - wire_rows
                main = jnp.zeros((chans, LANES), F32)
                for t in range(cols // 32):
                    main = jnp.where(lane // 32 == t, roll(w[8 * t + j], 32 * t - cols), main)
            rim = jnp.where(edge, roll(border, cols - 4 * r), 0.0)
            out.append(jnp.where(lane < cols, main, rim))
        g[block, 2 : 2 + rows] = row_pad(jnp.stack(out)).astype(BF16)

    unpack(c)
    for t in range(nc - 1):
        for up in (True, False):
            for h in range(2):

                @pl.when(arrives(up, t))
                def _():
                    z_arrival(up, t, h).wait_recv()

                if t + 1 < nc - 1:

                    @pl.when(sends(up, t + 1))
                    def _():
                        z_copy(up, t + 1, h).start()

        for up in (True, False):

            @pl.when(arrives(up, t))
            def _():
                unpack(c - 1 - t if up else c + 1 + t)

    def g_row(r):
        return jnp.concatenate([g[block, r] for block in range(nc)], axis=0)

    def f_row(r):
        return jnp.concatenate(
            [fa[a, r + 2 * b] for a in range(3) for b in range(3)], axis=0
        )

    acc = jnp.zeros((9 * PAD, nq), F32)
    for r in range(0, rows, 2):
        acc = acc + lax.dot_general(
            jnp.concatenate([f_row(r), f_row(r + 1)], axis=1),
            jnp.concatenate([g_row(r + 2), g_row(r + 3)], axis=1),
            (((1,), (1,)), ((), ())),
            preferred_element_type=F32,
        )
    acc = acc.reshape(9, PAD, nq)[:, :chans]
    tiles = jnp.concatenate(
        [
            acc[:, :, l * LANES : (l + 1) * LANES].reshape(9 * chans // 8, 8, LANES)
            for l in range(nq // LANES)
        ],
        axis=0,
    )
    n_tiles = tiles.shape[0]
    each = parts.shape[1]
    spare = ns * each - n_tiles
    if spare:
        tiles = jnp.concatenate([tiles, jnp.zeros((spare, 8, LANES), F32)], axis=0)
    parts[...] = tiles.reshape(ns, each, 8, LANES)

    def rs_copy(d):
        t = lax.rem(s + d, ns)
        return pltpu.make_async_remote_copy(
            src_ref=parts.at[t],
            dst_ref=rs.at[d - 1],
            send_sem=rs_send.at[d - 1],
            recv_sem=rs_recv.at[d - 1],
            device_id={"space": t, "chan": c},
            device_id_type=MESH,
        )

    def ag_copy(d):
        t = lax.rem(s + d, ns)
        return pltpu.make_async_remote_copy(
            src_ref=total.at[s],
            dst_ref=total.at[s],
            send_sem=ag_send.at[d - 1],
            recv_sem=ag_recv.at[d - 1],
            device_id={"space": t, "chan": c},
            device_id_type=MESH,
        )

    def ag_arrival(d):
        t = lax.rem(s + ns - d, ns)
        return pltpu.make_async_remote_copy(
            src_ref=total.at[t],
            dst_ref=total.at[t],
            send_sem=ag_send.at[d - 1],
            recv_sem=ag_recv.at[d - 1],
            device_id={"space": t, "chan": c},
            device_id_type=MESH,
        )

    for d in range(1, ns):
        rs_copy(d).start()

    def field_rows(first):
        out = []
        for r in range(first, first + 8, 2):
            operand = jnp.concatenate(
                [
                    jnp.concatenate([g_row(r + 4 - 2 * b), g_row(r + 5 - 2 * b)], axis=1)
                    for b in range(3)
                ],
                axis=0,
            )
            p = jnp.dot(wm[...], operand, preferred_element_type=F32)
            for j in range(2):
                part = p[:, j * LANES : (j + 1) * LANES]
                out.append(
                    sum(
                        roll(part[a * chans : (a + 1) * chans], 2 * (a - 1)) if a != 1
                        else part[a * chans : (a + 1) * chans]
                        for a in range(3)
                    )
                )
        out = jnp.swapaxes(jnp.stack(out), 0, 1)
        gf_ref[:, first : first + 8, :] = out[:, :, :cols]

    middle = rows // 2
    for first in range(0, middle, 8):
        field_rows(first)

    mine_total = parts[s]
    for d in range(1, ns):
        rs_copy(d).wait_recv()
        mine_total = mine_total + rs[d - 1]
    total[s] = mine_total * scale
    for d in range(1, ns):
        ag_copy(d).start()

    for first in range(middle, rows, 8):
        field_rows(first)

    for d in range(1, ns):
        ag_arrival(d).wait_recv()
    tiles = total[...].reshape(ns * each, 8, LANES)
    group = 9 * chans // 8
    per_lane = [
        tiles[l * group : (l + 1) * group].reshape(9, chans, LANES) for l in range(nq // LANES)
    ]
    spaced = per_lane[0] if len(per_lane) == 1 else jnp.concatenate(per_lane, axis=2)
    gw_ref[...] = jnp.concatenate(
        [spaced[:, :, b * PAD : b * PAD + chans] for b in range(nc)], axis=2
    )

    for t in range(nc - 1):
        for up in (True, False):

            @pl.when(sends(up, t))
            def _():
                for h in range(2):
                    z_copy(up, t, h).wait_send()

    for right, there in ((True, has_right), (False, has_left)):

        @pl.when(there)
        def _():
            for chan in range(nc):
                halo_copy(right, chan).wait_send()

    for d in range(1, ns):
        rs_copy(d).wait_send()
        ag_copy(d).wait_send()


def per_device(ns, nc, field, grad_out, filters):
    chans, cols, rows = field.shape
    wire_rows = rows * cols // LANES
    nq = nc * PAD
    ch = filters.shape[1]
    n_tiles = (9 * chans // 8) * (nq // LANES)
    each = -(-n_tiles // ns)
    scale = 1.0 / math.sqrt(rows * cols * ns)
    vmem = pl.BlockSpec(memory_space=pltpu.VMEM)
    dma = pltpu.SemaphoreType.DMA
    gf, gw = pl.pallas_call(
        functools.partial(kernel, ns, nc, scale),
        out_shape=(
            jax.ShapeDtypeStruct((chans, rows, cols), F32),
            jax.ShapeDtypeStruct((9, chans, ch), F32),
        ),
        in_specs=[vmem] * 3,
        out_specs=(vmem, vmem),
        scratch_shapes=[
            pltpu.VMEM((chans, rows, LANES), F32),
            pltpu.VMEM((nc, 2, wire_rows // 2 * chans, LANES), BF16),
            pltpu.VMEM((PAD, LANES), BF16),
            pltpu.VMEM((2, nc, PAD, LANES), BF16),
            pltpu.VMEM((nc, rows + 4, PAD, LANES), BF16),
            pltpu.VMEM((3, rows + 4, PAD, LANES), BF16),
            pltpu.VMEM((3 * chans, 3 * nq), BF16),
            pltpu.VMEM((ns, each, 8, LANES), F32),
            pltpu.VMEM((ns - 1, each, 8, LANES), F32),
            pltpu.VMEM((ns, each, 8, LANES), F32),
            dma((2, nc - 1, 2)),
            dma((2, nc - 1, 2)),
            dma((2, nc)),
            dma((2, nc)),
            dma((ns - 1,)),
            dma((ns - 1,)),
            dma((ns - 1,)),
            dma((ns - 1,)),
        ],
        compiler_params=pltpu.CompilerParams(
            collective_id=0, has_side_effects=True, vmem_limit_bytes=40 * 1024 * 1024
        ),
        cost_estimate=pl.CostEstimate(
            flops=4 * 9 * chans * ch * rows * cols, bytes_accessed=2 * 1024 * 1024, transcendentals=0
        ),
    )(jnp.swapaxes(field, 1, 2), jnp.swapaxes(grad_out, 1, 2), filters)
    return jnp.swapaxes(gf, 1, 2), gw


def solution(mesh):
    ns, nc = mesh.shape["space"], mesh.shape["chan"]
    in_specs = (P("chan", "space", None), P("chan", "space", None), P())
    out_specs = (P("chan", "space", None), P(None, "chan", None))
    return jax.shard_map(
        functools.partial(per_device, ns, nc),
        mesh=mesh, in_specs=in_specs, out_specs=out_specs, check_vma=False,
    )
```

```python
import functools
import math

import jax
import jax.numpy as jnp
from jax import lax
from jax.experimental import pallas as pl
from jax.experimental.pallas import tpu as pltpu
from jax.sharding import PartitionSpec as P

MESH = pl.DeviceIdType.MESH
F32 = jnp.float32
BF16 = jnp.bfloat16
LANES = 128
PAD = 32


def lane_index(shape):
    return lax.broadcasted_iota(jnp.int32, shape, len(shape) - 1)


def roll(x, shift):
    return pltpu.roll(x, shift % LANES, x.ndim - 1)


def row_pad(x):
    rows, chans, lanes = x.shape
    return jnp.concatenate([x, jnp.zeros((rows, PAD - chans, lanes), x.dtype)], axis=1)


def kernel(
    ns, nc, scale,
    field_hbm, grad_hbm, filt_hbm, gf_ref, gw_ref,
    field_ref, grad_ref, filt_ref,
    wide, wire, halo_own, halo_in, g, fa, wm, field_acc, parts, rs, total,
    in_sem, z_send, z_recv, h_send, h_recv, rs_send, rs_recv, ag_send, ag_recv,
):
    s = lax.axis_index("space")
    c = lax.axis_index("chan")
    chans, rows, cols = field_ref.shape
    loads = [
        pltpu.make_async_copy(src, dst, in_sem.at[i])
        for i, (src, dst) in enumerate(
            ((grad_hbm, grad_ref), (field_hbm, field_ref), (filt_hbm, filt_ref))
        )
    ]
    for load in loads:
        load.start()
    wire_rows = rows * cols // LANES
    half = wire_rows // 2
    nq = nc * PAD
    has_left, has_right = s > 0, s < ns - 1
    has_below, has_above = c > 0, c < nc - 1

    barrier = pltpu.get_barrier_semaphore()

    def greet(space, chan):
        pl.semaphore_signal(
            barrier, inc=1, device_id={"space": space, "chan": chan}, device_id_type=MESH
        )

    for d in range(1, ns):
        greet(lax.rem(s + d, ns), c)
    for d in range(1, nc):
        other = lax.rem(c + d, nc)

        @pl.when(has_left)
        def _():
            greet(s - 1, other)

        @pl.when(has_right)
        def _():
            greet(s + 1, other)

    @pl.when(has_below)
    def _():
        greet(s, c - 1)

    @pl.when(has_above)
    def _():
        greet(s, c + 1)

    wide[...] = jnp.zeros_like(wide)
    loads[0].wait()
    wide[:, :, :cols] = grad_ref[...].astype(F32)
    x = wide[...]
    lane = lane_index((chans, 8, LANES))
    tail = x[:, wire_rows:, :]
    packed = jnp.concatenate(
        [
            jnp.where(lane < cols, x[:, 8 * t : 8 * t + 8, :], roll(tail, cols - 32 * t))
            for t in range(wire_rows // 8)
        ],
        axis=1,
    )
    packed = jnp.swapaxes(packed, 0, 1)
    for h in range(2):
        wire[c, h] = packed[h * half : (h + 1) * half].reshape(half * chans, LANES).astype(BF16)

    lane = lane_index(x.shape)
    y = jnp.where(lane < 2, x, 0.0) + roll(
        jnp.where((lane >= cols - 2) & (lane < cols), x, 0.0), 30 - (cols - 2)
    )
    y = jnp.swapaxes(y, 0, 1)
    count = rows
    while count > 1:
        count //= 2
        y = y[:count] + roll(y[count:], 4 * count)
    halo_own[...] = row_pad(y)[0].astype(BF16)

    greeted = (ns - 1) + (nc - 1) * (
        has_left.astype(jnp.int32) + has_right.astype(jnp.int32)
    ) + has_below.astype(jnp.int32) + has_above.astype(jnp.int32)
    pl.semaphore_wait(barrier, greeted)

    def z_copy(up, t, h):
        block = c - t if up else c + t
        way = 0 if up else 1
        return pltpu.make_async_remote_copy(
            src_ref=wire.at[block, h],
            dst_ref=wire.at[block, h],
            send_sem=z_send.at[way, t, h],
            recv_sem=z_recv.at[way, t, h],
            device_id={"space": s, "chan": c + 1 if up else c - 1},
            device_id_type=MESH,
        )

    def z_arrival(up, t, h):
        block = c - 1 - t if up else c + 1 + t
        way = 0 if up else 1
        return pltpu.make_async_remote_copy(
            src_ref=wire.at[block, h],
            dst_ref=wire.at[block, h],
            send_sem=z_send.at[way, t, h],
            recv_sem=z_recv.at[way, t, h],
            device_id={"space": s, "chan": c - 1 if up else c + 1},
            device_id_type=MESH,
        )

    def sends(up, t):
        if up:
            return has_above & (c - t >= 0)
        return has_below & (c + t < nc)

    def arrives(up, t):
        if up:
            return c - 1 - t >= 0
        return c + 1 + t < nc

    def halo_copy(right, chan):
        side = 0 if right else 1
        return pltpu.make_async_remote_copy(
            src_ref=halo_own,
            dst_ref=halo_in.at[side, c],
            send_sem=h_send.at[side, chan],
            recv_sem=h_recv.at[side, c],
            device_id={"space": s + 1 if right else s - 1, "chan": chan},
            device_id_type=MESH,
        )

    def halo_arrival(side, block):
        return pltpu.make_async_remote_copy(
            src_ref=halo_own,
            dst_ref=halo_in.at[side, block],
            send_sem=h_send.at[side, block],
            recv_sem=h_recv.at[side, block],
            device_id={"space": s - 1 if side == 0 else s + 1, "chan": block},
            device_id_type=MESH,
        )

    for h in range(2):
        for up in (True, False):

            @pl.when(sends(up, 0))
            def _():
                z_copy(up, 0, h).start()

    for right, there in ((True, has_right), (False, has_left)):

        @pl.when(there)
        def _():
            for chan in range(nc):
                halo_copy(right, chan).start()

    for side, there in ((0, has_left), (1, has_right)):

        @pl.when(jnp.logical_not(there))
        def _():
            halo_in[side] = jnp.zeros_like(halo_in[side])

    loads[1].wait()
    wide[:, :, :cols] = field_ref[...].astype(F32)
    f = jnp.swapaxes(wide[...], 0, 1)
    for a in range(3):
        fa[a] = row_pad(roll(f, -2 * (a - 1))).astype(BF16)

    loads[2].wait()
    ch = filt_ref.shape[1]
    mine = lax.broadcasted_iota(jnp.int32, (chans, ch), 0) + c * chans
    pick = (mine == lane_index((chans, ch))).astype(F32).astype(BF16)
    q = lane_index((ch, nq))
    from_q = (q // PAD) * chans + lax.rem(q, PAD)
    spread = (
        (from_q == lax.broadcasted_iota(jnp.int32, (ch, nq), 0)) & (lax.rem(q, PAD) < chans)
    ).astype(F32).astype(BF16)
    taps = [
        jnp.dot(pick, filt_ref[k], preferred_element_type=F32) for k in range(9)
    ]
    taps = jnp.concatenate(taps, axis=0).astype(BF16)
    taps = jnp.dot(taps, spread, preferred_element_type=F32)
    for block in range(nc):
        own = taps[:, block * PAD : (block + 1) * PAD]
        wm[block] = jnp.concatenate(
            [
                jnp.concatenate(
                    [own[(3 * a + b) * chans : (3 * a + b + 1) * chans] for b in range(3)], axis=1
                )
                for a in range(3)
            ],
            axis=0,
        ).astype(BF16)

    for block in range(nc):
        g[block, 0:2] = jnp.zeros((2, PAD, LANES), BF16)
        g[block, rows + 2 :] = jnp.zeros((2, PAD, LANES), BF16)

    def unpack(block):
        for side, there in ((0, has_left), (1, has_right)):

            @pl.when(there)
            def _():
                halo_arrival(side, block).wait_recv()

        w = jnp.concatenate(
            [wire[block, h].astype(F32).reshape(half, chans, LANES) for h in range(2)], axis=0
        )
        lane = lane_index((chans, LANES))
        left = halo_in[0, block].astype(F32)[:chans]
        right = halo_in[1, block].astype(F32)[:chans]
        border = jnp.where(lane % 4 < 2, right, left)
        edge = ((lane >= cols) & (lane < cols + 2)) | (lane >= LANES - 2)
        out = []
        for r in range(rows):
            if r < wire_rows:
                main = w[r]
            else:
                j = r - wire_rows
                main = jnp.zeros((chans, LANES), F32)
                for t in range(cols // 32):
                    main = jnp.where(lane // 32 == t, roll(w[8 * t + j], 32 * t - cols), main)
            rim = jnp.where(edge, roll(border, cols - 4 * r), 0.0)
            out.append(jnp.where(lane < cols, main, rim))
        g[block, 2 : 2 + rows] = row_pad(jnp.stack(out)).astype(BF16)

    def g_pair(block, r):
        return jnp.concatenate(
            [
                jnp.concatenate([g[block, r + 4 - 2 * b], g[block, r + 5 - 2 * b]], axis=1)
                for b in range(3)
            ],
            axis=0,
        )

    n_tiles = 3 * chans // 8
    each = rs.shape[1]

    def weight_gradient(block):
        acc = jnp.zeros((3 * PAD, 3 * PAD), F32)
        for r in range(0, rows, 2):
            f_pair = jnp.concatenate(
                [jnp.concatenate([fa[a, r], fa[a, r + 1]], axis=1) for a in range(3)], axis=0
            )
            acc = acc + lax.dot_general(
                f_pair, g_pair(block, r), (((1,), (1,)), ((), ())), preferred_element_type=F32
            )
        acc = acc.reshape(3, PAD, 3 * PAD)[:, :chans].reshape(n_tiles, 8, 3 * PAD)
        acc = jnp.concatenate([acc, jnp.zeros((n_tiles, 8, LANES - 3 * PAD), F32)], axis=2)
        parts[pl.ds(block * n_tiles, n_tiles)] = acc

    def field_gradient(block, first=False):
        w = wm[block]
        for r in range(0, rows, 2):
            p = jnp.dot(w, g_pair(block, r), preferred_element_type=F32)
            field_acc[r // 2] = p if first else field_acc[r // 2] + p

    spare = ns * each - nc * n_tiles
    if spare:
        parts[nc * n_tiles :] = jnp.zeros((spare, 8, LANES), F32)

    def rs_copy(d):
        t = lax.rem(s + d, ns)
        return pltpu.make_async_remote_copy(
            src_ref=parts.at[pl.ds(t * each, each)],
            dst_ref=rs.at[d - 1],
            send_sem=rs_send.at[d - 1],
            recv_sem=rs_recv.at[d - 1],
            device_id={"space": t, "chan": c},
            device_id_type=MESH,
        )

    def ag_copy(d):
        t = lax.rem(s + d, ns)
        return pltpu.make_async_remote_copy(
            src_ref=total.at[s],
            dst_ref=total.at[s],
            send_sem=ag_send.at[d - 1],
            recv_sem=ag_recv.at[d - 1],
            device_id={"space": t, "chan": c},
            device_id_type=MESH,
        )

    def ag_arrival(d):
        t = lax.rem(s + ns - d, ns)
        return pltpu.make_async_remote_copy(
            src_ref=total.at[t],
            dst_ref=total.at[t],
            send_sem=ag_send.at[d - 1],
            recv_sem=ag_recv.at[d - 1],
            device_id={"space": t, "chan": c},
            device_id_type=MESH,
        )

    unpack(c)
    weight_gradient(c)
    field_gradient(c, first=True)
    for t in range(nc - 1):
        for h in range(2):
            for up in (True, False):

                @pl.when(arrives(up, t))
                def _():
                    z_arrival(up, t, h).wait_recv()

                if t + 1 < nc - 1:

                    @pl.when(sends(up, t + 1))
                    def _():
                        z_copy(up, t + 1, h).start()

        for up in (True, False):

            @pl.when(arrives(up, t))
            def _():
                block = c - 1 - t if up else c + 1 + t
                unpack(block)
                weight_gradient(block)

        if t + 1 == nc - 1:
            for d in range(1, ns):
                rs_copy(d).start()

        for up in (True, False):

            @pl.when(arrives(up, t))
            def _():
                field_gradient(c - 1 - t if up else c + 1 + t)

    def field_rows(first):
        out = []
        for r in range(first, first + 8, 2):
            p = field_acc[r // 2]
            for j in range(2):
                part = p[:, j * LANES : (j + 1) * LANES]
                out.append(
                    sum(
                        roll(part[a * chans : (a + 1) * chans], 2 * (a - 1)) if a != 1
                        else part[a * chans : (a + 1) * chans]
                        for a in range(3)
                    )
                )
        out = jnp.swapaxes(jnp.stack(out), 0, 1)
        gf_ref[:, first : first + 8, :] = out[:, :, :cols]

    middle = rows // 2
    for first in range(0, middle, 8):
        field_rows(first)

    mine_total = parts[pl.ds(s * each, each)]
    for d in range(1, ns):
        rs_copy(d).wait_recv()
        mine_total = mine_total + rs[d - 1]
    total[s] = mine_total * scale
    for d in range(1, ns):
        ag_copy(d).start()

    for first in range(middle, rows, 8):
        field_rows(first)

    for d in range(1, ns):
        ag_arrival(d).wait_recv()
    tiles = total[...].reshape(ns * each, 8, LANES)
    blocks = [
        tiles[b * n_tiles : (b + 1) * n_tiles].reshape(3, chans, LANES) for b in range(nc)
    ]
    for a in range(3):
        for b in range(3):
            gw_ref[3 * a + b] = jnp.concatenate(
                [block[a, :, b * PAD : b * PAD + chans] for block in blocks], axis=1
            )

    for t in range(nc - 1):
        for up in (True, False):

            @pl.when(sends(up, t))
            def _():
                for h in range(2):
                    z_copy(up, t, h).wait_send()

    for right, there in ((True, has_right), (False, has_left)):

        @pl.when(there)
        def _():
            for chan in range(nc):
                halo_copy(right, chan).wait_send()

    for d in range(1, ns):
        rs_copy(d).wait_send()
        ag_copy(d).wait_send()


def per_device(ns, nc, field, grad_out, filters):
    chans, cols, rows = field.shape
    wire_rows = rows * cols // LANES
    ch = filters.shape[1]
    n_tiles = nc * 3 * chans // 8
    each = -(-n_tiles // ns)
    scale = 1.0 / math.sqrt(rows * cols * ns)
    vmem = pl.BlockSpec(memory_space=pltpu.VMEM)
    dma = pltpu.SemaphoreType.DMA
    gf, gw = pl.pallas_call(
        functools.partial(kernel, ns, nc, scale),
        out_shape=(
            jax.ShapeDtypeStruct((chans, rows, cols), F32),
            jax.ShapeDtypeStruct((9, chans, ch), F32),
        ),
        in_specs=[pl.BlockSpec(memory_space=pltpu.HBM)] * 3,
        out_specs=(vmem, vmem),
        scratch_shapes=[
            pltpu.VMEM((chans, rows, cols), BF16),
            pltpu.VMEM((chans, rows, cols), BF16),
            pltpu.VMEM(filters.shape, BF16),
            pltpu.VMEM((chans, rows, LANES), F32),
            pltpu.VMEM((nc, 2, wire_rows // 2 * chans, LANES), BF16),
            pltpu.VMEM((PAD, LANES), BF16),
            pltpu.VMEM((2, nc, PAD, LANES), BF16),
            pltpu.VMEM((nc, rows + 4, PAD, LANES), BF16),
            pltpu.VMEM((3, rows, PAD, LANES), BF16),
            pltpu.VMEM((nc, 3 * chans, 3 * PAD), BF16),
            pltpu.VMEM((rows // 2, 3 * chans, 2 * LANES), F32),
            pltpu.VMEM((ns * each, 8, LANES), F32),
            pltpu.VMEM((ns - 1, each, 8, LANES), F32),
            pltpu.VMEM((ns, each, 8, LANES), F32),
            dma((3,)),
            dma((2, nc - 1, 2)),
            dma((2, nc - 1, 2)),
            dma((2, nc)),
            dma((2, nc)),
            dma((ns - 1,)),
            dma((ns - 1,)),
            dma((ns - 1,)),
            dma((ns - 1,)),
        ],
        compiler_params=pltpu.CompilerParams(
            collective_id=0, has_side_effects=True, vmem_limit_bytes=64 * 1024 * 1024
        ),
        cost_estimate=pl.CostEstimate(
            flops=4 * 9 * chans * ch * rows * cols, bytes_accessed=2 * 1024 * 1024, transcendentals=0
        ),
    )(jnp.swapaxes(field, 1, 2), jnp.swapaxes(grad_out, 1, 2), filters)
    return jnp.swapaxes(gf, 1, 2), gw


def solution(mesh):
    ns, nc = mesh.shape["space"], mesh.shape["chan"]
    in_specs = (P("chan", "space", None), P("chan", "space", None), P())
    out_specs = (P("chan", "space", None), P(None, "chan", None))
    return jax.shard_map(
        functools.partial(per_device, ns, nc),
        mesh=mesh, in_specs=in_specs, out_specs=out_specs, check_vma=False,
    )
```

```python
import functools
import math

import jax
import jax.numpy as jnp
from jax import lax
from jax.experimental import pallas as pl
from jax.experimental.pallas import tpu as pltpu
from jax.sharding import PartitionSpec as P

MESH = pl.DeviceIdType.MESH
F32 = jnp.float32
BF16 = jnp.bfloat16
LANES = 128
PAD = 32


def lane_index(shape):
    return lax.broadcasted_iota(jnp.int32, shape, len(shape) - 1)


def roll(x, shift):
    return pltpu.roll(x, shift % LANES, x.ndim - 1)


def row_pad(x):
    rows, chans, lanes = x.shape
    return jnp.concatenate([x, jnp.zeros((rows, PAD - chans, lanes), x.dtype)], axis=1)


def kernel(
    ns, nc, scale,
    field_hbm, grad_hbm, filt_hbm, gf_hbm, gw_hbm,
    field_ref, grad_ref, filt_ref, gf_ref, gw_ref,
    wide, wire, halo_own, halo_in, g, fa, wm, field_acc, parts, rs, total,
    in_sem, out_sem, z_send, z_recv, h_send, h_recv, rs_send, rs_recv, ag_send, ag_recv,
):
    s = lax.axis_index("space")
    c = lax.axis_index("chan")
    chans, rows, cols = field_ref.shape
    loads = [
        pltpu.make_async_copy(src, dst, in_sem.at[i])
        for i, (src, dst) in enumerate(
            ((grad_hbm, grad_ref), (field_hbm, field_ref), (filt_hbm, filt_ref))
        )
    ]
    for load in loads:
        load.start()
    span = rows // 2
    half = span * cols // LANES
    nq = nc * PAD
    has_left, has_right = s > 0, s < ns - 1
    has_below, has_above = c > 0, c < nc - 1

    barrier = pltpu.get_barrier_semaphore()

    def greet(space, chan):
        pl.semaphore_signal(
            barrier, inc=1, device_id={"space": space, "chan": chan}, device_id_type=MESH
        )

    for d in range(1, ns):
        greet(lax.rem(s + d, ns), c)
    for d in range(1, nc):
        other = lax.rem(c + d, nc)

        @pl.when(has_left)
        def _():
            greet(s - 1, other)

        @pl.when(has_right)
        def _():
            greet(s + 1, other)

    @pl.when(has_below)
    def _():
        greet(s, c - 1)

    @pl.when(has_above)
    def _():
        greet(s, c + 1)

    wide[...] = jnp.zeros_like(wide)
    loads[0].wait()
    wide[:, :, :cols] = grad_ref[...].astype(F32)
    x = wide[...]
    y = jnp.swapaxes(x, 0, 1)
    lane = lane_index((chans, LANES))
    left_over = span - half
    for h in range(2):
        packed = [
            jnp.where(
                lane < cols,
                y[span * h + i],
                roll(y[span * h + half + i % left_over], cols - 32 * (i // left_over)),
            )
            for i in range(half)
        ]
        wire[c, h] = jnp.stack(packed).reshape(half * chans, LANES).astype(BF16)

    greeted = (ns - 1) + (nc - 1) * (
        has_left.astype(jnp.int32) + has_right.astype(jnp.int32)
    ) + has_below.astype(jnp.int32) + has_above.astype(jnp.int32)
    pl.semaphore_wait(barrier, greeted)

    def z_copy(up, t, h):
        block = c - t if up else c + t
        way = 0 if up else 1
        return pltpu.make_async_remote_copy(
            src_ref=wire.at[block, h],
            dst_ref=wire.at[block, h],
            send_sem=z_send.at[way, t, h],
            recv_sem=z_recv.at[way, t, h],
            device_id={"space": s, "chan": c + 1 if up else c - 1},
            device_id_type=MESH,
        )

    def z_arrival(up, t, h):
        block = c - 1 - t if up else c + 1 + t
        way = 0 if up else 1
        return pltpu.make_async_remote_copy(
            src_ref=wire.at[block, h],
            dst_ref=wire.at[block, h],
            send_sem=z_send.at[way, t, h],
            recv_sem=z_recv.at[way, t, h],
            device_id={"space": s, "chan": c - 1 if up else c + 1},
            device_id_type=MESH,
        )

    def sends(up, t):
        if up:
            return has_above & (c - t >= 0)
        return has_below & (c + t < nc)

    def arrives(up, t):
        if up:
            return c - 1 - t >= 0
        return c + 1 + t < nc

    def halo_copy(right, chan):
        side = 0 if right else 1
        return pltpu.make_async_remote_copy(
            src_ref=halo_own,
            dst_ref=halo_in.at[side, c],
            send_sem=h_send.at[side, chan],
            recv_sem=h_recv.at[side, c],
            device_id={"space": s + 1 if right else s - 1, "chan": chan},
            device_id_type=MESH,
        )

    def halo_arrival(side, block):
        return pltpu.make_async_remote_copy(
            src_ref=halo_own,
            dst_ref=halo_in.at[side, block],
            send_sem=h_send.at[side, block],
            recv_sem=h_recv.at[side, block],
            device_id={"space": s - 1 if side == 0 else s + 1, "chan": block},
            device_id_type=MESH,
        )

    for h in range(2):
        for up in (True, False):

            @pl.when(sends(up, 0))
            def _():
                z_copy(up, 0, h).start()

    place = lane_index(y.shape)
    y = jnp.where(place < 2, y, 0.0) + roll(
        jnp.where((place >= cols - 2) & (place < cols), y, 0.0), 30 - (cols - 2)
    )
    count = rows
    while count > 1:
        count //= 2
        y = y[:count] + roll(y[count:], 4 * count)
    halo_own[...] = row_pad(y)[0].astype(BF16)

    for right, there in ((True, has_right), (False, has_left)):

        @pl.when(there)
        def _():
            for chan in range(nc):
                halo_copy(right, chan).start()

    for side, there in ((0, has_left), (1, has_right)):

        @pl.when(jnp.logical_not(there))
        def _():
            halo_in[side] = jnp.zeros_like(halo_in[side])

    loads[1].wait()
    wide[:, :, :cols] = field_ref[...].astype(F32)
    f = jnp.swapaxes(wide[...], 0, 1)
    for a in range(3):
        fa[a] = row_pad(roll(f, -2 * (a - 1))).astype(BF16)

    loads[2].wait()
    ch = filt_ref.shape[1]
    mine = lax.broadcasted_iota(jnp.int32, (chans, ch), 0) + c * chans
    pick = (mine == lane_index((chans, ch))).astype(F32).astype(BF16)
    q = lane_index((ch, nq))
    from_q = (q // PAD) * chans + lax.rem(q, PAD)
    spread = (
        (from_q == lax.broadcasted_iota(jnp.int32, (ch, nq), 0)) & (lax.rem(q, PAD) < chans)
    ).astype(F32).astype(BF16)
    taps = [
        jnp.dot(pick, filt_ref[k], preferred_element_type=F32) for k in range(9)
    ]
    taps = jnp.concatenate(taps, axis=0).astype(BF16)
    taps = jnp.dot(taps, spread, preferred_element_type=F32)
    for block in range(nc):
        own = taps[:, block * PAD : (block + 1) * PAD]
        wm[block] = jnp.concatenate(
            [
                jnp.concatenate(
                    [own[(3 * a + b) * chans : (3 * a + b + 1) * chans] for b in range(3)], axis=1
                )
                for a in range(3)
            ],
            axis=0,
        ).astype(BF16)

    for block in range(nc):
        g[block, 0:2] = jnp.zeros((2, PAD, LANES), BF16)
        g[block, rows + 2 :] = jnp.zeros((2, PAD, LANES), BF16)

    def unpack(block, h):
        if h == 0:
            for side, there in ((0, has_left), (1, has_right)):

                @pl.when(there)
                def _():
                    halo_arrival(side, block).wait_recv()

        w = wire[block, h].astype(F32).reshape(half, chans, LANES)
        left = halo_in[0, block].astype(F32)[:chans]
        right = halo_in[1, block].astype(F32)[:chans]
        border = jnp.where(lane % 4 < 2, right, left)
        edge = ((lane >= cols) & (lane < cols + 2)) | (lane >= LANES - 2)
        placed = []
        for i in range(span):
            if i < half:
                main = w[i]
            else:
                main = roll(w[i - half], -cols)
                for t in range(1, cols // 32):
                    main = jnp.where(
                        lane // 32 == t, roll(w[left_over * t + i - half], 32 * t - cols), main
                    )
            rim = jnp.where(edge, roll(border, cols - 4 * (span * h + i)), 0.0)
            placed.append(jnp.where(lane < cols, main, rim))
        g[block, 2 + span * h : 2 + span * (h + 1)] = row_pad(jnp.stack(placed)).astype(BF16)

    def ready(h):
        return range(0, span - 2, 2) if h == 0 else range(span - 2, rows, 2)

    def g_pair(block, r):
        return jnp.concatenate(
            [
                jnp.concatenate([g[block, r + 4 - 2 * b], g[block, r + 5 - 2 * b]], axis=1)
                for b in range(3)
            ],
            axis=0,
        )

    n_tiles = 3 * chans // 8
    each = rs.shape[1]

    def weight_gradient(block, h):
        acc = jnp.zeros((3 * PAD, 3 * PAD), F32)
        for r in ready(h):
            f_pair = jnp.concatenate(
                [jnp.concatenate([fa[a, r], fa[a, r + 1]], axis=1) for a in range(3)], axis=0
            )
            acc = acc + lax.dot_general(
                f_pair, g_pair(block, r), (((1,), (1,)), ((), ())), preferred_element_type=F32
            )
        acc = acc.reshape(3, PAD, 3 * PAD)[:, :chans].reshape(n_tiles, 8, 3 * PAD)
        acc = jnp.concatenate([acc, jnp.zeros((n_tiles, 8, LANES - 3 * PAD), F32)], axis=2)
        at = pl.ds(block * n_tiles, n_tiles)
        parts[at] = acc if h == 0 else parts[at] + acc

    def field_gradient(block, h, first=False):
        w = wm[block]
        for r in ready(h):
            p = jnp.dot(w, g_pair(block, r), preferred_element_type=F32)
            field_acc[r // 2] = p if first else field_acc[r // 2] + p

    spare = ns * each - nc * n_tiles
    if spare:
        parts[nc * n_tiles :] = jnp.zeros((spare, 8, LANES), F32)

    def rs_copy(d):
        t = lax.rem(s + d, ns)
        return pltpu.make_async_remote_copy(
            src_ref=parts.at[pl.ds(t * each, each)],
            dst_ref=rs.at[d - 1],
            send_sem=rs_send.at[d - 1],
            recv_sem=rs_recv.at[d - 1],
            device_id={"space": t, "chan": c},
            device_id_type=MESH,
        )

    def ag_copy(d):
        t = lax.rem(s + d, ns)
        return pltpu.make_async_remote_copy(
            src_ref=total.at[s],
            dst_ref=total.at[s],
            send_sem=ag_send.at[d - 1],
            recv_sem=ag_recv.at[d - 1],
            device_id={"space": t, "chan": c},
            device_id_type=MESH,
        )

    def ag_arrival(d):
        t = lax.rem(s + ns - d, ns)
        return pltpu.make_async_remote_copy(
            src_ref=total.at[t],
            dst_ref=total.at[t],
            send_sem=ag_send.at[d - 1],
            recv_sem=ag_recv.at[d - 1],
            device_id={"space": t, "chan": c},
            device_id_type=MESH,
        )

    def work(block, h):
        unpack(block, h)
        weight_gradient(block, h)
        field_gradient(block, h)

    def both(t):
        return arrives(True, t) & arrives(False, t)

    def first_block(t):
        above = c + 1 + t
        return above - arrives(True, t).astype(jnp.int32) * (2 * t + 2)

    for t in range(nc - 1):
        any_here = arrives(True, t) | arrives(False, t)
        passes_on = sends(True, t + 1) | sends(False, t + 1)
        late = t > 0 and 2 * (t - 1) <= nc - 3
        last = t == nc - 2
        for h in range(2):
            for up in (True, False):

                @pl.when(arrives(up, t))
                def _():
                    z_arrival(up, t, h).wait_recv()

                if not last:

                    @pl.when(sends(up, t + 1))
                    def _():
                        z_copy(up, t + 1, h).start()

            if t == 0:
                unpack(c, h)
                weight_gradient(c, h)
                field_gradient(c, h, first=True)
            if late:

                @pl.when(both(t - 1))
                def _():
                    work(c + t, h)

            if t > 0 and h == 0:

                @pl.when(any_here if last else any_here & jnp.logical_not(passes_on))
                def _():
                    work(first_block(t), 0)

        if t == 0 or not last:

            @pl.when(any_here if t == 0 else any_here & passes_on)
            def _():
                work(first_block(t), 0)

        @pl.when(any_here)
        def _():
            unpack(first_block(t), 1)
            weight_gradient(first_block(t), 1)

        if last:
            for d in range(1, ns):
                rs_copy(d).start()

        @pl.when(any_here)
        def _():
            field_gradient(first_block(t), 1)

    def field_rows(first):
        out = []
        for r in range(first, first + 8, 2):
            p = field_acc[r // 2]
            for j in range(2):
                part = p[:, j * LANES : (j + 1) * LANES]
                out.append(
                    sum(
                        roll(part[a * chans : (a + 1) * chans], 2 * (a - 1)) if a != 1
                        else part[a * chans : (a + 1) * chans]
                        for a in range(3)
                    )
                )
        out = jnp.swapaxes(jnp.stack(out), 0, 1)
        gf_ref[:, first : first + 8, :] = out[:, :, :cols]

    middle = rows // 2
    def gf_out(i):
        at = pl.ds(i * middle, middle)
        return pltpu.make_async_copy(gf_ref.at[:, at], gf_hbm.at[:, at], out_sem.at[i])

    for first in range(0, middle, 8):
        field_rows(first)
    gf_out(0).start()

    mine_total = parts[pl.ds(s * each, each)]
    for d in range(1, ns):
        rs_copy(d).wait_recv()
        mine_total = mine_total + rs[d - 1]
    total[s] = mine_total * scale
    for d in range(1, ns):
        ag_copy(d).start()

    for first in range(middle, rows, 8):
        field_rows(first)
    gf_out(1).start()

    for d in range(1, ns):
        ag_arrival(d).wait_recv()
    tiles = total[...].reshape(ns * each, 8, LANES)
    blocks = [
        tiles[b * n_tiles : (b + 1) * n_tiles].reshape(3, chans, LANES) for b in range(nc)
    ]
    for a in range(3):
        for b in range(3):
            gw_ref[3 * a + b] = jnp.concatenate(
                [block[a, :, b * PAD : b * PAD + chans] for block in blocks], axis=1
            )

    gw_out = pltpu.make_async_copy(gw_ref, gw_hbm, out_sem.at[2])
    gw_out.start()

    for t in range(nc - 1):
        for up in (True, False):

            @pl.when(sends(up, t))
            def _():
                for h in range(2):
                    z_copy(up, t, h).wait_send()

    for right, there in ((True, has_right), (False, has_left)):

        @pl.when(there)
        def _():
            for chan in range(nc):
                halo_copy(right, chan).wait_send()

    for d in range(1, ns):
        rs_copy(d).wait_send()
        ag_copy(d).wait_send()
    gf_out(0).wait()
    gf_out(1).wait()
    gw_out.wait()


def keep(gf_in, gw_in, gf_out, gw_out, sem):
    copies = [
        pltpu.make_async_copy(gf_in, gf_out, sem.at[0]),
        pltpu.make_async_copy(gw_in, gw_out, sem.at[1]),
    ]
    for copy in copies:
        copy.start()
    for copy in copies:
        copy.wait()


def per_device(ns, nc, field, grad_out, filters):
    chans, cols, rows = field.shape
    ch = filters.shape[1]
    n_tiles = nc * 3 * chans // 8
    each = -(-n_tiles // ns)
    scale = 1.0 / math.sqrt(rows * cols * ns)
    hbm = pl.BlockSpec(memory_space=pltpu.HBM)
    dma = pltpu.SemaphoreType.DMA
    gf, gw = pl.pallas_call(
        functools.partial(kernel, ns, nc, scale),
        out_shape=(
            jax.ShapeDtypeStruct((chans, rows, cols), F32),
            jax.ShapeDtypeStruct((9, chans, ch), F32),
        ),
        in_specs=[hbm] * 3,
        out_specs=(hbm, hbm),
        scratch_shapes=[
            pltpu.VMEM((chans, rows, cols), BF16),
            pltpu.VMEM((chans, rows, cols), BF16),
            pltpu.VMEM(filters.shape, BF16),
            pltpu.VMEM((chans, rows, cols), F32),
            pltpu.VMEM((9, chans, ch), F32),
            pltpu.VMEM((chans, rows, LANES), F32),
            pltpu.VMEM((nc, 2, rows // 2 * cols // LANES * chans, LANES), BF16),
            pltpu.VMEM((PAD, LANES), BF16),
            pltpu.VMEM((2, nc, PAD, LANES), BF16),
            pltpu.VMEM((nc, rows + 4, PAD, LANES), BF16),
            pltpu.VMEM((3, rows, PAD, LANES), BF16),
            pltpu.VMEM((nc, 3 * chans, 3 * PAD), BF16),
            pltpu.VMEM((rows // 2, 3 * chans, 2 * LANES), F32),
            pltpu.VMEM((ns * each, 8, LANES), F32),
            pltpu.VMEM((ns - 1, each, 8, LANES), F32),
            pltpu.VMEM((ns, each, 8, LANES), F32),
            dma((3,)),
            dma((3,)),
            dma((2, nc - 1, 2)),
            dma((2, nc - 1, 2)),
            dma((2, nc)),
            dma((2, nc)),
            dma((ns - 1,)),
            dma((ns - 1,)),
            dma((ns - 1,)),
            dma((ns - 1,)),
        ],
        compiler_params=pltpu.CompilerParams(
            collective_id=0, has_side_effects=True, vmem_limit_bytes=64 * 1024 * 1024
        ),
        cost_estimate=pl.CostEstimate(
            flops=4 * 9 * chans * ch * rows * cols, bytes_accessed=2 * 1024 * 1024, transcendentals=0
        ),
    )(jnp.swapaxes(field, 1, 2), jnp.swapaxes(grad_out, 1, 2), filters)
    gf, gw = pl.pallas_call(
        keep,
        out_shape=(
            jax.ShapeDtypeStruct(gf.shape, F32),
            jax.ShapeDtypeStruct(gw.shape, F32),
        ),
        in_specs=[hbm] * 2,
        out_specs=(hbm, hbm),
        scratch_shapes=[dma((2,))],
        compiler_params=pltpu.CompilerParams(vmem_limit_bytes=64 * 1024 * 1024),
    )(gf, gw)
    return jnp.swapaxes(gf, 1, 2), gw


def solution(mesh):
    ns, nc = mesh.shape["space"], mesh.shape["chan"]
    in_specs = (P("chan", "space", None), P("chan", "space", None), P())
    out_specs = (P("chan", "space", None), P(None, "chan", None))
    return jax.shard_map(
        functools.partial(per_device, ns, nc),
        mesh=mesh, in_specs=in_specs, out_specs=out_specs, check_vma=False,
    )
```

```python
import functools
import math

import jax
import jax.numpy as jnp
from jax import lax
from jax.experimental import pallas as pl
from jax.experimental.pallas import tpu as pltpu
from jax.sharding import PartitionSpec as P

MESH = pl.DeviceIdType.MESH
F32 = jnp.float32
BF16 = jnp.bfloat16
LANES = 128
PAD = 32


def lane_index(shape):
    return lax.broadcasted_iota(jnp.int32, shape, len(shape) - 1)


def roll(x, shift):
    return pltpu.roll(x, shift % LANES, x.ndim - 1)


def row_pad(x):
    rows, chans, lanes = x.shape
    return jnp.concatenate([x, jnp.zeros((rows, PAD - chans, lanes), x.dtype)], axis=1)


def kernel(
    ns, nc, scale,
    field_hbm, grad_hbm, filt_hbm, gf_hbm, gw_hbm,
    field_ref, grad_ref, filt_ref, gf_ref, gw_ref,
    wide, wire, halo_own, halo_in, g, fa, wm, field_acc, parts, rs, total,
    in_sem, out_sem, z_send, z_recv, h_send, h_recv, rs_send, rs_recv, ag_send, ag_recv,
):
    s = lax.axis_index("space")
    c = lax.axis_index("chan")
    chans, rows, cols = field_ref.shape
    loads = [
        pltpu.make_async_copy(src, dst, in_sem.at[i])
        for i, (src, dst) in enumerate(
            ((grad_hbm, grad_ref), (field_hbm, field_ref), (filt_hbm, filt_ref))
        )
    ]
    for load in loads:
        load.start()
    span = rows // 2
    half = span * cols // LANES
    nq = nc * PAD
    has_left, has_right = s > 0, s < ns - 1
    has_below, has_above = c > 0, c < nc - 1

    barrier = pltpu.get_barrier_semaphore()

    def greet(space, chan):
        pl.semaphore_signal(
            barrier, inc=1, device_id={"space": space, "chan": chan}, device_id_type=MESH
        )

    for d in range(1, ns):
        greet(lax.rem(s + d, ns), c)
    for d in range(1, nc):
        other = lax.rem(c + d, nc)

        @pl.when(has_left)
        def _():
            greet(s - 1, other)

        @pl.when(has_right)
        def _():
            greet(s + 1, other)

    @pl.when(has_below)
    def _():
        greet(s, c - 1)

    @pl.when(has_above)
    def _():
        greet(s, c + 1)

    wide[...] = jnp.zeros_like(wide)
    loads[0].wait()
    wide[:, :, :cols] = grad_ref[...].astype(F32)
    x = wide[...]
    y = jnp.swapaxes(x, 0, 1)
    lane = lane_index((chans, LANES))
    left_over = span - half
    for h in range(2):
        packed = [
            jnp.where(
                lane < cols,
                y[span * h + i],
                roll(y[span * h + half + i % left_over], cols - 32 * (i // left_over)),
            )
            for i in range(half)
        ]
        wire[c, h] = jnp.stack(packed).reshape(half * chans, LANES).astype(BF16)

    greeted = (ns - 1) + (nc - 1) * (
        has_left.astype(jnp.int32) + has_right.astype(jnp.int32)
    ) + has_below.astype(jnp.int32) + has_above.astype(jnp.int32)
    pl.semaphore_wait(barrier, greeted)

    def z_copy(up, t, h):
        block = c - t if up else c + t
        way = 0 if up else 1
        return pltpu.make_async_remote_copy(
            src_ref=wire.at[block, h],
            dst_ref=wire.at[block, h],
            send_sem=z_send.at[way, t, h],
            recv_sem=z_recv.at[way, t, h],
            device_id={"space": s, "chan": c + 1 if up else c - 1},
            device_id_type=MESH,
        )

    def z_arrival(up, t, h):
        block = c - 1 - t if up else c + 1 + t
        way = 0 if up else 1
        return pltpu.make_async_remote_copy(
            src_ref=wire.at[block, h],
            dst_ref=wire.at[block, h],
            send_sem=z_send.at[way, t, h],
            recv_sem=z_recv.at[way, t, h],
            device_id={"space": s, "chan": c - 1 if up else c + 1},
            device_id_type=MESH,
        )

    def sends(up, t):
        if up:
            return has_above & (c - t >= 0)
        return has_below & (c + t < nc)

    def arrives(up, t):
        if up:
            return c - 1 - t >= 0
        return c + 1 + t < nc

    def halo_copy(right, chan):
        side = 0 if right else 1
        return pltpu.make_async_remote_copy(
            src_ref=halo_own,
            dst_ref=halo_in.at[side, c],
            send_sem=h_send.at[side, chan],
            recv_sem=h_recv.at[side, c],
            device_id={"space": s + 1 if right else s - 1, "chan": chan},
            device_id_type=MESH,
        )

    def halo_arrival(side, block):
        return pltpu.make_async_remote_copy(
            src_ref=halo_own,
            dst_ref=halo_in.at[side, block],
            send_sem=h_send.at[side, block],
            recv_sem=h_recv.at[side, block],
            device_id={"space": s - 1 if side == 0 else s + 1, "chan": block},
            device_id_type=MESH,
        )

    for h in range(2):
        for up in (True, False):

            @pl.when(sends(up, 0))
            def _():
                z_copy(up, 0, h).start()

    place = lane_index(y.shape)
    y = jnp.where(place < 2, y, 0.0) + roll(
        jnp.where((place >= cols - 2) & (place < cols), y, 0.0), 30 - (cols - 2)
    )
    count = rows
    while count > 1:
        count //= 2
        y = y[:count] + roll(y[count:], 4 * count)
    halo_own[...] = row_pad(y)[0].astype(BF16)

    for right, there in ((True, has_right), (False, has_left)):

        @pl.when(there)
        def _():
            for chan in range(nc):
                halo_copy(right, chan).start()

    for side, there in ((0, has_left), (1, has_right)):

        @pl.when(jnp.logical_not(there))
        def _():
            halo_in[side] = jnp.zeros_like(halo_in[side])

    loads[1].wait()
    wide[:, :, :cols] = field_ref[...].astype(F32)
    f = jnp.swapaxes(wide[...], 0, 1)
    for a in range(3):
        fa[a] = row_pad(roll(f, -2 * (a - 1))).astype(BF16)

    loads[2].wait()
    ch = filt_ref.shape[1]
    mine = lax.broadcasted_iota(jnp.int32, (chans, ch), 0) + c * chans
    pick = (mine == lane_index((chans, ch))).astype(F32).astype(BF16)
    q = lane_index((ch, nq))
    from_q = (q // PAD) * chans + lax.rem(q, PAD)
    spread = (
        (from_q == lax.broadcasted_iota(jnp.int32, (ch, nq), 0)) & (lax.rem(q, PAD) < chans)
    ).astype(F32).astype(BF16)
    taps = [
        jnp.dot(pick, filt_ref[k], preferred_element_type=F32) for k in range(9)
    ]
    taps = jnp.concatenate(taps, axis=0).astype(BF16)
    taps = jnp.dot(taps, spread, preferred_element_type=F32)
    for block in range(nc):
        own = taps[:, block * PAD : (block + 1) * PAD]
        wm[block] = jnp.concatenate(
            [
                jnp.concatenate(
                    [own[(3 * a + b) * chans : (3 * a + b + 1) * chans] for b in range(3)], axis=1
                )
                for a in range(3)
            ],
            axis=0,
        ).astype(BF16)

    for block in range(nc):
        g[block, 0:2] = jnp.zeros((2, PAD, LANES), BF16)
        g[block, rows + 2 :] = jnp.zeros((2, PAD, LANES), BF16)

    def unpack(block, h):
        if h == 0:
            for side, there in ((0, has_left), (1, has_right)):

                @pl.when(there)
                def _():
                    halo_arrival(side, block).wait_recv()

        w = wire[block, h].astype(F32).reshape(half, chans, LANES)
        left = halo_in[0, block].astype(F32)[:chans]
        right = halo_in[1, block].astype(F32)[:chans]
        border = jnp.where(lane % 4 < 2, right, left)
        edge = ((lane >= cols) & (lane < cols + 2)) | (lane >= LANES - 2)
        placed = []
        for i in range(span):
            if i < half:
                main = w[i]
            else:
                main = roll(w[i - half], -cols)
                for t in range(1, cols // 32):
                    main = jnp.where(
                        lane // 32 == t, roll(w[left_over * t + i - half], 32 * t - cols), main
                    )
            rim = jnp.where(edge, roll(border, cols - 4 * (span * h + i)), 0.0)
            placed.append(jnp.where(lane < cols, main, rim))
        g[block, 2 + span * h : 2 + span * (h + 1)] = row_pad(jnp.stack(placed)).astype(BF16)

    def ready(h):
        return range(0, span - 2) if h == 0 else range(span - 2, rows)

    def g_rows(block, h):
        return jnp.concatenate(
            [
                jnp.concatenate([g[block, r + 4 - 2 * b] for r in ready(h)], axis=1)
                for b in range(3)
            ],
            axis=0,
        )

    def f_rows(h):
        return jnp.concatenate(
            [jnp.concatenate([fa[a, r] for r in ready(h)], axis=1) for a in range(3)], axis=0
        )

    n_tiles = 3 * chans // 8
    each = rs.shape[1]

    def weight_gradient(block, h):
        acc = lax.dot_general(
            f_rows(h), g_rows(block, h), (((1,), (1,)), ((), ())), preferred_element_type=F32
        )
        acc = acc.reshape(3, PAD, 3 * PAD)[:, :chans].reshape(n_tiles, 8, 3 * PAD)
        acc = jnp.concatenate([acc, jnp.zeros((n_tiles, 8, LANES - 3 * PAD), F32)], axis=2)
        at = pl.ds(block * n_tiles, n_tiles)
        parts[at] = acc if h == 0 else parts[at] + acc

    def field_gradient(block, h, first=False):
        p = jnp.dot(wm[block], g_rows(block, h), preferred_element_type=F32)
        for i, r in enumerate(ready(h)):
            here = p[:, i * LANES : (i + 1) * LANES]
            field_acc[r] = here if first else field_acc[r] + here

    spare = ns * each - nc * n_tiles
    if spare:
        parts[nc * n_tiles :] = jnp.zeros((spare, 8, LANES), F32)

    def rs_copy(d):
        t = lax.rem(s + d, ns)
        return pltpu.make_async_remote_copy(
            src_ref=parts.at[pl.ds(t * each, each)],
            dst_ref=rs.at[d - 1],
            send_sem=rs_send.at[d - 1],
            recv_sem=rs_recv.at[d - 1],
            device_id={"space": t, "chan": c},
            device_id_type=MESH,
        )

    def ag_copy(d):
        t = lax.rem(s + d, ns)
        return pltpu.make_async_remote_copy(
            src_ref=total.at[s],
            dst_ref=total.at[s],
            send_sem=ag_send.at[d - 1],
            recv_sem=ag_recv.at[d - 1],
            device_id={"space": t, "chan": c},
            device_id_type=MESH,
        )

    def ag_arrival(d):
        t = lax.rem(s + ns - d, ns)
        return pltpu.make_async_remote_copy(
            src_ref=total.at[t],
            dst_ref=total.at[t],
            send_sem=ag_send.at[d - 1],
            recv_sem=ag_recv.at[d - 1],
            device_id={"space": t, "chan": c},
            device_id_type=MESH,
        )

    def work(block, h):
        unpack(block, h)
        weight_gradient(block, h)
        field_gradient(block, h)

    def both(t):
        return arrives(True, t) & arrives(False, t)

    def first_block(t):
        above = c + 1 + t
        return above - arrives(True, t).astype(jnp.int32) * (2 * t + 2)

    for t in range(nc - 1):
        any_here = arrives(True, t) | arrives(False, t)
        passes_on = sends(True, t + 1) | sends(False, t + 1)
        late = t > 0 and 2 * (t - 1) <= nc - 3
        last = t == nc - 2
        for h in range(2):
            for up in (True, False):

                @pl.when(arrives(up, t))
                def _():
                    z_arrival(up, t, h).wait_recv()

                if not last:

                    @pl.when(sends(up, t + 1))
                    def _():
                        z_copy(up, t + 1, h).start()

            if t == 0:
                unpack(c, h)
                weight_gradient(c, h)
                field_gradient(c, h, first=True)
            if late:

                @pl.when(both(t - 1))
                def _():
                    work(c + t, h)

            if t > 0 and h == 0:

                @pl.when(any_here if last else any_here & jnp.logical_not(passes_on))
                def _():
                    work(first_block(t), 0)

        if t == 0 or not last:

            @pl.when(any_here if t == 0 else any_here & passes_on)
            def _():
                work(first_block(t), 0)

        @pl.when(any_here)
        def _():
            unpack(first_block(t), 1)
            weight_gradient(first_block(t), 1)

        if last:
            for d in range(1, ns):
                rs_copy(d).start()

        @pl.when(any_here)
        def _():
            field_gradient(first_block(t), 1)

    def field_rows(first):
        out = []
        for r in range(first, first + 8):
            p = field_acc[r]
            out.append(
                roll(p[:chans], -2) + p[chans : 2 * chans] + roll(p[2 * chans :], 2)
            )
        out = jnp.swapaxes(jnp.stack(out), 0, 1)
        gf_ref[:, first : first + 8, :] = out[:, :, :cols]

    middle = rows // 2
    def gf_out(i):
        at = pl.ds(i * middle, middle)
        return pltpu.make_async_copy(gf_ref.at[:, at], gf_hbm.at[:, at], out_sem.at[i])

    for first in range(0, middle, 8):
        field_rows(first)
    gf_out(0).start()

    mine_total = parts[pl.ds(s * each, each)]
    for d in range(1, ns):
        rs_copy(d).wait_recv()
        mine_total = mine_total + rs[d - 1]
    total[s] = mine_total * scale
    for d in range(1, ns):
        ag_copy(d).start()

    for first in range(middle, rows, 8):
        field_rows(first)
    gf_out(1).start()

    for d in range(1, ns):
        ag_arrival(d).wait_recv()
    tiles = total[...].reshape(ns * each, 8, LANES)
    blocks = [
        tiles[b * n_tiles : (b + 1) * n_tiles].reshape(3, chans, LANES) for b in range(nc)
    ]
    for a in range(3):
        for b in range(3):
            gw_ref[3 * a + b] = jnp.concatenate(
                [block[a, :, b * PAD : b * PAD + chans] for block in blocks], axis=1
            )

    gw_out = pltpu.make_async_copy(gw_ref, gw_hbm, out_sem.at[2])
    gw_out.start()

    for t in range(nc - 1):
        for up in (True, False):

            @pl.when(sends(up, t))
            def _():
                for h in range(2):
                    z_copy(up, t, h).wait_send()

    for right, there in ((True, has_right), (False, has_left)):

        @pl.when(there)
        def _():
            for chan in range(nc):
                halo_copy(right, chan).wait_send()

    for d in range(1, ns):
        rs_copy(d).wait_send()
        ag_copy(d).wait_send()
    gf_out(0).wait()
    gf_out(1).wait()
    gw_out.wait()


def keep(gf_in, gw_in, gf_out, gw_out, gf, gw, in_sem, out_sem):
    pieces = in_sem.shape[0] - 1
    step = gf.shape[0] // pieces
    ins, outs = [], []
    for i in range(pieces):
        at = pl.ds(i * step, step)
        ins.append(pltpu.make_async_copy(gf_in.at[at], gf.at[at], in_sem.at[i]))
        outs.append(pltpu.make_async_copy(gf.at[at], gf_out.at[at], out_sem.at[i]))
    ins.append(pltpu.make_async_copy(gw_in, gw, in_sem.at[pieces]))
    outs.append(pltpu.make_async_copy(gw, gw_out, out_sem.at[pieces]))
    for copy in ins:
        copy.start()
    for there, back in zip(ins, outs):
        there.wait()
        back.start()
    for copy in outs:
        copy.wait()


def per_device(ns, nc, field, grad_out, filters):
    chans, cols, rows = field.shape
    ch = filters.shape[1]
    n_tiles = nc * 3 * chans // 8
    each = -(-n_tiles // ns)
    scale = 1.0 / math.sqrt(rows * cols * ns)
    hbm = pl.BlockSpec(memory_space=pltpu.HBM)
    dma = pltpu.SemaphoreType.DMA
    gf, gw = pl.pallas_call(
        functools.partial(kernel, ns, nc, scale),
        out_shape=(
            jax.ShapeDtypeStruct((chans, rows, cols), F32),
            jax.ShapeDtypeStruct((9, chans, ch), F32),
        ),
        in_specs=[hbm] * 3,
        out_specs=(hbm, hbm),
        scratch_shapes=[
            pltpu.VMEM((chans, rows, cols), BF16),
            pltpu.VMEM((chans, rows, cols), BF16),
            pltpu.VMEM(filters.shape, BF16),
            pltpu.VMEM((chans, rows, cols), F32),
            pltpu.VMEM((9, chans, ch), F32),
            pltpu.VMEM((chans, rows, LANES), F32),
            pltpu.VMEM((nc, 2, rows // 2 * cols // LANES * chans, LANES), BF16),
            pltpu.VMEM((PAD, LANES), BF16),
            pltpu.VMEM((2, nc, PAD, LANES), BF16),
            pltpu.VMEM((nc, rows + 4, PAD, LANES), BF16),
            pltpu.VMEM((3, rows, PAD, LANES), BF16),
            pltpu.VMEM((nc, 3 * chans, 3 * PAD), BF16),
            pltpu.VMEM((rows, 3 * chans, LANES), F32),
            pltpu.VMEM((ns * each, 8, LANES), F32),
            pltpu.VMEM((ns - 1, each, 8, LANES), F32),
            pltpu.VMEM((ns, each, 8, LANES), F32),
            dma((3,)),
            dma((3,)),
            dma((2, nc - 1, 2)),
            dma((2, nc - 1, 2)),
            dma((2, nc)),
            dma((2, nc)),
            dma((ns - 1,)),
            dma((ns - 1,)),
            dma((ns - 1,)),
            dma((ns - 1,)),
        ],
        compiler_params=pltpu.CompilerParams(
            collective_id=0, has_side_effects=True, vmem_limit_bytes=64 * 1024 * 1024
        ),
        cost_estimate=pl.CostEstimate(
            flops=4 * 9 * chans * ch * rows * cols, bytes_accessed=2 * 1024 * 1024, transcendentals=0
        ),
    )(jnp.swapaxes(field, 1, 2), jnp.swapaxes(grad_out, 1, 2), filters)
    gf, gw = pl.pallas_call(
        keep,
        out_shape=(
            jax.ShapeDtypeStruct(gf.shape, F32),
            jax.ShapeDtypeStruct(gw.shape, F32),
        ),
        in_specs=[hbm] * 2,
        out_specs=(hbm, hbm),
        scratch_shapes=[
            pltpu.VMEM(gf.shape, F32), pltpu.VMEM(gw.shape, F32), dma((4,)), dma((4,)),
        ],
        compiler_params=pltpu.CompilerParams(vmem_limit_bytes=64 * 1024 * 1024),
    )(gf, gw)
    return jnp.swapaxes(gf, 1, 2), gw


def solution(mesh):
    ns, nc = mesh.shape["space"], mesh.shape["chan"]
    in_specs = (P("chan", "space", None), P("chan", "space", None), P())
    out_specs = (P("chan", "space", None), P(None, "chan", None))
    return jax.shard_map(
        functools.partial(per_device, ns, nc),
        mesh=mesh, in_specs=in_specs, out_specs=out_specs, check_vma=False,
    )
```

```python
import functools
import math

import jax
import jax.numpy as jnp
from jax import lax
from jax.experimental import pallas as pl
from jax.experimental.pallas import tpu as pltpu
from jax.sharding import PartitionSpec as P

MESH = pl.DeviceIdType.MESH
F32 = jnp.float32
BF16 = jnp.bfloat16
LANES = 128
PAD = 32


def lane_index(shape):
    return lax.broadcasted_iota(jnp.int32, shape, len(shape) - 1)


def roll(x, shift):
    return pltpu.roll(x, shift % LANES, x.ndim - 1)


def row_pad(x):
    rows, chans, lanes = x.shape
    return jnp.concatenate([x, jnp.zeros((rows, PAD - chans, lanes), x.dtype)], axis=1)


def kernel(
    ns, nc, scale,
    field_hbm, grad_hbm, filt_hbm, gf_hbm, gw_hbm,
    field_ref, grad_ref, filt_ref, gf_ref, gw_ref,
    wide, wire, halo_own, halo_in, g, fa, wm, field_acc, parts, rs, total,
    in_sem, out_sem, z_send, z_recv, h_send, h_recv, rs_send, rs_recv, ag_send, ag_recv,
):
    s = lax.axis_index("space")
    c = lax.axis_index("chan")
    chans, rows, cols = field_ref.shape
    loads = [
        pltpu.make_async_copy(src, dst, in_sem.at[i])
        for i, (src, dst) in enumerate(
            ((grad_hbm, grad_ref), (field_hbm, field_ref), (filt_hbm, filt_ref))
        )
    ]
    for load in loads:
        load.start()
    span = rows // 2
    half = span * cols // LANES
    nq = nc * PAD
    has_left, has_right = s > 0, s < ns - 1
    has_below, has_above = c > 0, c < nc - 1

    barrier = pltpu.get_barrier_semaphore()

    def greet(space, chan):
        pl.semaphore_signal(
            barrier, inc=1, device_id={"space": space, "chan": chan}, device_id_type=MESH
        )

    for d in range(1, ns):
        greet(lax.rem(s + d, ns), c)
    for d in range(1, nc):
        other = lax.rem(c + d, nc)

        @pl.when(has_left)
        def _():
            greet(s - 1, other)

        @pl.when(has_right)
        def _():
            greet(s + 1, other)

    @pl.when(has_below)
    def _():
        greet(s, c - 1)

    @pl.when(has_above)
    def _():
        greet(s, c + 1)

    wide[...] = jnp.zeros_like(wide)
    loads[0].wait()
    wide[:, :, :cols] = grad_ref[...].astype(F32)
    x = wide[...]
    y = jnp.swapaxes(x, 0, 1)
    lane = lane_index((chans, LANES))
    left_over = span - half
    for h in range(2):
        packed = [
            jnp.where(
                lane < cols,
                y[span * h + i],
                roll(y[span * h + half + i % left_over], cols - 32 * (i // left_over)),
            )
            for i in range(half)
        ]
        wire[c, h] = jnp.stack(packed).reshape(half * chans, LANES).astype(BF16)

    greeted = (ns - 1) + (nc - 1) * (
        has_left.astype(jnp.int32) + has_right.astype(jnp.int32)
    ) + has_below.astype(jnp.int32) + has_above.astype(jnp.int32)
    pl.semaphore_wait(barrier, greeted)

    def z_copy(up, t, h):
        block = c - t if up else c + t
        way = 0 if up else 1
        return pltpu.make_async_remote_copy(
            src_ref=wire.at[block, h],
            dst_ref=wire.at[block, h],
            send_sem=z_send.at[way, t, h],
            recv_sem=z_recv.at[way, t, h],
            device_id={"space": s, "chan": c + 1 if up else c - 1},
            device_id_type=MESH,
        )

    def z_arrival(up, t, h):
        block = c - 1 - t if up else c + 1 + t
        way = 0 if up else 1
        return pltpu.make_async_remote_copy(
            src_ref=wire.at[block, h],
            dst_ref=wire.at[block, h],
            send_sem=z_send.at[way, t, h],
            recv_sem=z_recv.at[way, t, h],
            device_id={"space": s, "chan": c - 1 if up else c + 1},
            device_id_type=MESH,
        )

    def sends(up, t):
        if up:
            return has_above & (c - t >= 0)
        return has_below & (c + t < nc)

    def arrives(up, t):
        if up:
            return c - 1 - t >= 0
        return c + 1 + t < nc

    def halo_copy(right, chan):
        side = 0 if right else 1
        return pltpu.make_async_remote_copy(
            src_ref=halo_own.at[side],
            dst_ref=halo_in.at[side, c],
            send_sem=h_send.at[side, chan],
            recv_sem=h_recv.at[side, c],
            device_id={"space": s + 1 if right else s - 1, "chan": chan},
            device_id_type=MESH,
        )

    def halo_arrival(side, block):
        return pltpu.make_async_remote_copy(
            src_ref=halo_own.at[side],
            dst_ref=halo_in.at[side, block],
            send_sem=h_send.at[side, block],
            recv_sem=h_recv.at[side, block],
            device_id={"space": s - 1 if side == 0 else s + 1, "chan": block},
            device_id_type=MESH,
        )

    for h in range(2):
        for up in (True, False):

            @pl.when(sends(up, 0))
            def _():
                z_copy(up, 0, h).start()

    place = lane_index(y.shape)
    y = jnp.where(place < 2, y, 0.0) + roll(
        jnp.where((place >= cols - 2) & (place < cols), y, 0.0), 30 - (cols - 2)
    )
    count = rows
    while count > 1:
        count //= 2
        y = y[:count] + roll(y[count:], 4 * count)
    ends = y[0]
    fold = halo_own.shape[1]
    filler = jnp.zeros((2 * fold - chans, LANES), F32)
    for side in range(2):
        kept = jnp.where((lane % 4 < 2) == (side == 1), ends, 0.0)
        rest = jnp.concatenate([roll(kept[fold:], 2 if side else -2), filler], axis=0)
        halo_own[side] = (kept[:fold] + rest).astype(BF16)

    for right, there in ((True, has_right), (False, has_left)):

        @pl.when(there)
        def _():
            for chan in range(nc):
                halo_copy(right, chan).start()

    for side, there in ((0, has_left), (1, has_right)):

        @pl.when(jnp.logical_not(there))
        def _():
            halo_in[side] = jnp.zeros_like(halo_in[side])

    loads[1].wait()
    wide[:, :, :cols] = field_ref[...].astype(F32)
    f = jnp.swapaxes(wide[...], 0, 1)
    for a in range(3):
        fa[a] = row_pad(roll(f, -2 * (a - 1))).astype(BF16)

    loads[2].wait()
    ch = filt_ref.shape[1]
    mine = lax.broadcasted_iota(jnp.int32, (chans, ch), 0) + c * chans
    pick = (mine == lane_index((chans, ch))).astype(F32).astype(BF16)
    q = lane_index((ch, nq))
    from_q = (q // PAD) * chans + lax.rem(q, PAD)
    spread = (
        (from_q == lax.broadcasted_iota(jnp.int32, (ch, nq), 0)) & (lax.rem(q, PAD) < chans)
    ).astype(F32).astype(BF16)
    taps = [
        jnp.dot(pick, filt_ref[k], preferred_element_type=F32) for k in range(9)
    ]
    taps = jnp.concatenate(taps, axis=0).astype(BF16)
    taps = jnp.dot(taps, spread, preferred_element_type=F32)
    for block in range(nc):
        own = taps[:, block * PAD : (block + 1) * PAD]
        wm[block] = jnp.concatenate(
            [
                jnp.concatenate(
                    [own[(3 * a + b) * chans : (3 * a + b + 1) * chans] for b in range(3)], axis=1
                )
                for a in range(3)
            ],
            axis=0,
        ).astype(BF16)

    for block in range(nc):
        g[block, 0:2] = jnp.zeros((2, PAD, LANES), BF16)
        g[block, rows + 2 :] = jnp.zeros((2, PAD, LANES), BF16)

    def unpack(block, h):
        if h == 0:
            for side, there in ((0, has_left), (1, has_right)):

                @pl.when(there)
                def _():
                    halo_arrival(side, block).wait_recv()

        w = wire[block, h].astype(F32).reshape(half, chans, LANES)
        left, right = halo_in[0, block].astype(F32), halo_in[1, block].astype(F32)
        more = chans - left.shape[0]
        left = jnp.concatenate([left, roll(left[:more], 2)], axis=0)
        right = jnp.concatenate([right, roll(right[:more], -2)], axis=0)
        border = jnp.where(lane % 4 < 2, right, left)
        edge = ((lane >= cols) & (lane < cols + 2)) | (lane >= LANES - 2)
        placed = []
        for i in range(span):
            if i < half:
                main = w[i]
            else:
                main = roll(w[i - half], -cols)
                for t in range(1, cols // 32):
                    main = jnp.where(
                        lane // 32 == t, roll(w[left_over * t + i - half], 32 * t - cols), main
                    )
            rim = jnp.where(edge, roll(border, cols - 4 * (span * h + i)), 0.0)
            placed.append(jnp.where(lane < cols, main, rim))
        g[block, 2 + span * h : 2 + span * (h + 1)] = row_pad(jnp.stack(placed)).astype(BF16)

    def ready(h):
        return range(0, span - 2) if h == 0 else range(span - 2, rows)

    def g_rows(block, h):
        return jnp.concatenate(
            [
                jnp.concatenate([g[block, r + 4 - 2 * b] for r in ready(h)], axis=1)
                for b in range(3)
            ],
            axis=0,
        )

    def f_rows(h):
        return jnp.concatenate(
            [jnp.concatenate([fa[a, r] for r in ready(h)], axis=1) for a in range(3)], axis=0
        )

    n_tiles = 3 * chans // 8
    each = rs.shape[1]

    def weight_gradient(block, h):
        acc = lax.dot_general(
            f_rows(h), g_rows(block, h), (((1,), (1,)), ((), ())), preferred_element_type=F32
        )
        acc = acc.reshape(3, PAD, 3 * PAD)[:, :chans].reshape(n_tiles, 8, 3 * PAD)
        acc = jnp.concatenate([acc, jnp.zeros((n_tiles, 8, LANES - 3 * PAD), F32)], axis=2)
        at = pl.ds(block * n_tiles, n_tiles)
        parts[at] = acc if h == 0 else parts[at] + acc

    def field_gradient(block, h, first=False):
        p = jnp.dot(wm[block], g_rows(block, h), preferred_element_type=F32)
        for i, r in enumerate(ready(h)):
            here = p[:, i * LANES : (i + 1) * LANES]
            field_acc[r] = here if first else field_acc[r] + here

    spare = ns * each - nc * n_tiles
    if spare:
        parts[nc * n_tiles :] = jnp.zeros((spare, 8, LANES), F32)

    def rs_copy(d):
        t = lax.rem(s + d, ns)
        return pltpu.make_async_remote_copy(
            src_ref=parts.at[pl.ds(t * each, each)],
            dst_ref=rs.at[d - 1],
            send_sem=rs_send.at[d - 1],
            recv_sem=rs_recv.at[d - 1],
            device_id={"space": t, "chan": c},
            device_id_type=MESH,
        )

    def ag_copy(d):
        t = lax.rem(s + d, ns)
        return pltpu.make_async_remote_copy(
            src_ref=total.at[s],
            dst_ref=total.at[s],
            send_sem=ag_send.at[d - 1],
            recv_sem=ag_recv.at[d - 1],
            device_id={"space": t, "chan": c},
            device_id_type=MESH,
        )

    def ag_arrival(d):
        t = lax.rem(s + ns - d, ns)
        return pltpu.make_async_remote_copy(
            src_ref=total.at[t],
            dst_ref=total.at[t],
            send_sem=ag_send.at[d - 1],
            recv_sem=ag_recv.at[d - 1],
            device_id={"space": t, "chan": c},
            device_id_type=MESH,
        )

    def work(block, h):
        unpack(block, h)
        weight_gradient(block, h)
        field_gradient(block, h)

    def both(t):
        return arrives(True, t) & arrives(False, t)

    def first_block(t):
        above = c + 1 + t
        return above - arrives(True, t).astype(jnp.int32) * (2 * t + 2)

    for t in range(nc - 1):
        any_here = arrives(True, t) | arrives(False, t)
        passes_on = sends(True, t + 1) | sends(False, t + 1)
        late = t > 0 and 2 * (t - 1) <= nc - 3
        last = t == nc - 2
        for h in range(2):
            for up in (True, False):

                @pl.when(arrives(up, t))
                def _():
                    z_arrival(up, t, h).wait_recv()

                if not last:

                    @pl.when(sends(up, t + 1))
                    def _():
                        z_copy(up, t + 1, h).start()

            if t == 0:
                unpack(c, h)
                weight_gradient(c, h)
                field_gradient(c, h, first=True)
            if late:

                @pl.when(both(t - 1))
                def _():
                    work(c + t, h)

            if t > 0 and h == 0:

                @pl.when(any_here if last else any_here & jnp.logical_not(passes_on))
                def _():
                    work(first_block(t), 0)

        if t == 0 or not last:

            @pl.when(any_here if t == 0 else any_here & passes_on)
            def _():
                work(first_block(t), 0)

        @pl.when(any_here)
        def _():
            unpack(first_block(t), 1)
            weight_gradient(first_block(t), 1)

        if last:
            for d in range(1, ns):
                rs_copy(d).start()

        @pl.when(any_here)
        def _():
            field_gradient(first_block(t), 1)

    def field_rows(first):
        out = []
        for r in range(first, first + 8):
            p = field_acc[r]
            out.append(
                roll(p[:chans], -2) + p[chans : 2 * chans] + roll(p[2 * chans :], 2)
            )
        out = jnp.swapaxes(jnp.stack(out), 0, 1)
        gf_ref[:, first : first + 8, :] = out[:, :, :cols]

    middle = rows // 2
    def gf_out(i):
        at = pl.ds(i * middle, middle)
        return pltpu.make_async_copy(gf_ref.at[:, at], gf_hbm.at[:, at], out_sem.at[i])

    for first in range(0, middle, 8):
        field_rows(first)
    gf_out(0).start()

    mine_total = parts[pl.ds(s * each, each)]
    for d in range(1, ns):
        rs_copy(d).wait_recv()
        mine_total = mine_total + rs[d - 1]
    total[s] = mine_total * scale
    for d in range(1, ns):
        ag_copy(d).start()

    for first in range(middle, rows, 8):
        field_rows(first)
    gf_out(1).start()

    for d in range(1, ns):
        ag_arrival(d).wait_recv()
    tiles = total[...].reshape(ns * each, 8, LANES)
    blocks = [
        tiles[b * n_tiles : (b + 1) * n_tiles].reshape(3, chans, LANES) for b in range(nc)
    ]
    for a in range(3):
        for b in range(3):
            gw_ref[3 * a + b] = jnp.concatenate(
                [block[a, :, b * PAD : b * PAD + chans] for block in blocks], axis=1
            )

    gw_out = pltpu.make_async_copy(gw_ref, gw_hbm, out_sem.at[2])
    gw_out.start()

    for t in range(nc - 1):
        for up in (True, False):

            @pl.when(sends(up, t))
            def _():
                for h in range(2):
                    z_copy(up, t, h).wait_send()

    for right, there in ((True, has_right), (False, has_left)):

        @pl.when(there)
        def _():
            for chan in range(nc):
                halo_copy(right, chan).wait_send()

    for d in range(1, ns):
        rs_copy(d).wait_send()
        ag_copy(d).wait_send()
    gf_out(0).wait()
    gf_out(1).wait()
    gw_out.wait()


def keep(gf_in, gw_in, gf_out, gw_out, gf, gw, in_sem, out_sem):
    pieces = in_sem.shape[0] - 1
    step = gf.shape[0] // pieces
    ins, outs = [], []
    for i in range(pieces):
        at = pl.ds(i * step, step)
        ins.append(pltpu.make_async_copy(gf_in.at[at], gf.at[at], in_sem.at[i]))
        outs.append(pltpu.make_async_copy(gf.at[at], gf_out.at[at], out_sem.at[i]))
    ins.append(pltpu.make_async_copy(gw_in, gw, in_sem.at[pieces]))
    outs.append(pltpu.make_async_copy(gw, gw_out, out_sem.at[pieces]))
    for copy in ins:
        copy.start()
    for there, back in zip(ins, outs):
        there.wait()
        back.start()
    for copy in outs:
        copy.wait()


def per_device(ns, nc, field, grad_out, filters):
    chans, cols, rows = field.shape
    ch = filters.shape[1]
    n_tiles = nc * 3 * chans // 8
    each = -(-n_tiles // ns)
    scale = 1.0 / math.sqrt(rows * cols * ns)
    hbm = pl.BlockSpec(memory_space=pltpu.HBM)
    dma = pltpu.SemaphoreType.DMA
    gf, gw = pl.pallas_call(
        functools.partial(kernel, ns, nc, scale),
        out_shape=(
            jax.ShapeDtypeStruct((chans, rows, cols), F32),
            jax.ShapeDtypeStruct((9, chans, ch), F32),
        ),
        in_specs=[hbm] * 3,
        out_specs=(hbm, hbm),
        scratch_shapes=[
            pltpu.VMEM((chans, rows, cols), BF16),
            pltpu.VMEM((chans, rows, cols), BF16),
            pltpu.VMEM(filters.shape, BF16),
            pltpu.VMEM((chans, rows, cols), F32),
            pltpu.VMEM((9, chans, ch), F32),
            pltpu.VMEM((chans, rows, LANES), F32),
            pltpu.VMEM((nc, 2, rows // 2 * cols // LANES * chans, LANES), BF16),
            pltpu.VMEM((2, PAD // 2, LANES), BF16),
            pltpu.VMEM((2, nc, PAD // 2, LANES), BF16),
            pltpu.VMEM((nc, rows + 4, PAD, LANES), BF16),
            pltpu.VMEM((3, rows, PAD, LANES), BF16),
            pltpu.VMEM((nc, 3 * chans, 3 * PAD), BF16),
            pltpu.VMEM((rows, 3 * chans, LANES), F32),
            pltpu.VMEM((ns * each, 8, LANES), F32),
            pltpu.VMEM((ns - 1, each, 8, LANES), F32),
            pltpu.VMEM((ns, each, 8, LANES), F32),
            dma((3,)),
            dma((3,)),
            dma((2, nc - 1, 2)),
            dma((2, nc - 1, 2)),
            dma((2, nc)),
            dma((2, nc)),
            dma((ns - 1,)),
            dma((ns - 1,)),
            dma((ns - 1,)),
            dma((ns - 1,)),
        ],
        compiler_params=pltpu.CompilerParams(
            collective_id=0, has_side_effects=True, vmem_limit_bytes=64 * 1024 * 1024
        ),
        cost_estimate=pl.CostEstimate(
            flops=4 * 9 * chans * ch * rows * cols, bytes_accessed=2 * 1024 * 1024, transcendentals=0
        ),
    )(jnp.swapaxes(field, 1, 2), jnp.swapaxes(grad_out, 1, 2), filters)
    gf, gw = pl.pallas_call(
        keep,
        out_shape=(
            jax.ShapeDtypeStruct(gf.shape, F32),
            jax.ShapeDtypeStruct(gw.shape, F32),
        ),
        in_specs=[hbm] * 2,
        out_specs=(hbm, hbm),
        scratch_shapes=[
            pltpu.VMEM(gf.shape, F32), pltpu.VMEM(gw.shape, F32), dma((4,)), dma((4,)),
        ],
        compiler_params=pltpu.CompilerParams(vmem_limit_bytes=64 * 1024 * 1024),
    )(gf, gw)
    return jnp.swapaxes(gf, 1, 2), gw


def solution(mesh):
    ns, nc = mesh.shape["space"], mesh.shape["chan"]
    in_specs = (P("chan", "space", None), P("chan", "space", None), P())
    out_specs = (P("chan", "space", None), P(None, "chan", None))
    return jax.shard_map(
        functools.partial(per_device, ns, nc),
        mesh=mesh, in_specs=in_specs, out_specs=out_specs, check_vma=False,
    )
```
